128 devices in a mesh: ctx: 16 (over y, z), tp: 8 (over x, core).
Axes of the slice: x: 4, y: 4, z: 4, core: 2. Of those that a mesh axis runs over, the one named last changes fastest.
Arguments:
- query_proj: bfloat16 [8192, 8192], P('ctx', 'tp'), may hold values from -6 to 6
- key_proj: bfloat16 [8192, 8192], P('ctx', 'tp'), may hold values from -6 to 6
- value_proj: bfloat16 [8192, 8192], P('ctx', 'tp'), may hold values from -6 to 6
- filter_spectrum: bfloat16 [2, 16384, 8192], P(None, 'ctx', 'tp'), may hold values from -24 to 24
- skip_gain: float32 [8192], P('tp'), may hold values from 0.5 to 1.5
- out_weight: bfloat16 [8192, 8192], P('tp'), may hold values from -0.09375 to 0.09375
Outputs:
- block_out: bfloat16 [8192, 8192], P('ctx', 'tp')
The draws below stay inside these ranges and needn't reach their ends.
All inputs are finite; a program needn't handle non-finite values.
Results may differ from the reference program's by a relative error of at most 0.012.
Values may be sent and summed in bfloat16 or wider, within the bound.
No kernel may reach another device: no remote copies, remote signals or barrier semaphores. Data moves between devices by JAX's collectives and lax.ppermute only.
A program may use at most 128 MiB of HBM per device.

```python
import math
import jax
import jax.numpy as jnp
from jax import lax

WIDTH = 8192
SEQ = 8192
FFT_LEN = 16384


def draw_filter_spectrum(key, part):
    key = jax.random.fold_in(key, 7)
    keys = jax.random.split(key, 6)
    modes = 4
    limit = 24.0
    slow_share = 0.5
    noise = jax.random.truncated_normal(keys[5], -4.0, 4.0, (2, FFT_LEN, WIDTH), jnp.float32)
    noise_scale = jnp.exp(jax.random.uniform(keys[4], (WIDTH,), jnp.float32, math.log(0.3), math.log(3.0)))
    slow = jax.random.bernoulli(keys[0], slow_share, (modes, WIDTH))
    slow_rate = jnp.exp(jax.random.uniform(keys[1], (modes, WIDTH), jnp.float32, math.log(0.3 / SEQ), math.log(2.0 / SEQ)))
    fast_rate = jnp.exp(jax.random.uniform(keys[2], (modes, WIDTH), jnp.float32, math.log(1.0 / 50.0), math.log(1.0 / 30.0)))
    rates = jnp.where(slow, slow_rate, fast_rate)
    coefs = jax.random.truncated_normal(keys[3], -3.0, 3.0, (modes, WIDTH), jnp.float32) * jnp.sqrt(2.0 * rates / modes)
    freq = jnp.arange(FFT_LEN, dtype=jnp.int32)
    theta = (freq.astype(jnp.float32) * (2.0 * math.pi / FFT_LEN))[:, None]
    parity = (1 - 2 * (freq % 2)).astype(jnp.float32)[:, None]
    sin_theta = jnp.sin(theta)
    half_sin = jnp.sin(0.5 * theta)

    def add_mode(index, carry):
        real_sum, imag_sum = carry
        rate_row = rates[index][None, :]
        decay = jnp.exp(-rate_row)
        gap = -jnp.expm1(-rate_row)
        tail = jnp.exp(-rate_row * SEQ)
        top = coefs[index][None, :] * (1.0 - tail * parity)
        den_real = gap + 2.0 * decay * half_sin * half_sin
        den_imag = decay * sin_theta
        factor = top / (den_real * den_real + den_imag * den_imag)
        return (real_sum + factor * den_real, imag_sum - factor * den_imag)
    zeros = jnp.zeros((FFT_LEN, WIDTH), jnp.float32)
    real_sum, imag_sum = lax.fori_loop(0, modes, add_mode, (zeros, zeros))
    total = jnp.stack([real_sum, imag_sum]) + noise * noise_scale[None, None, :]
    return jnp.clip(total, -limit, limit).astype(jnp.bfloat16)


def spiked(array, own_key, source, target, parts, factor):
    def block_of(position):
        return (jnp.arange(array.shape[position]) // (array.shape[position] // parts)).reshape((-1,) + (1,) * (array.ndim - 1 - position))

    near = jax.random.permutation(own_key, parts)[block_of(target)]
    second = (block_of(target) + parts // 2) % parts
    return jnp.where((block_of(source) == near) | (block_of(source) == second), factor * array, array)


def steps_of(own_key, extent, cuts, low, high):
    level, own = 1.0, jax.random.fold_in(own_key, 6)
    for dim, shards_of in cuts:
        heights = jnp.exp(jax.random.uniform(jax.random.fold_in(own, dim), (shards_of,), jnp.float32, low / len(cuts), high / len(cuts)))
        level = level * jnp.repeat(heights, extent[dim] // shards_of).reshape([-1 if axis == dim else 1 for axis in range(len(extent))])
    return level


def gaussian(own_key, dims, deviation, most, cuts=(), held_as=jnp.bfloat16):
    array = deviation * jax.random.normal(own_key, dims, jnp.float32)
    if cuts:
        array = array * steps_of(own_key, dims, cuts, -0.22, 0.18)
    return jnp.clip(array, -most, most).astype(held_as)


def noise_with(rng, dims, width, bound, shards, heavy, kind=jnp.bfloat16):
    array = width * jax.random.normal(rng, dims, jnp.float32)
    if shards:
        array = array * steps_of(rng, dims, shards, -0.22, 0.18)
    return jnp.clip(spiked(array, jax.random.fold_in(rng, 3), *heavy), -bound, bound).astype(kind)


def setup_inputs(seed: int = 0) -> dict:
    splits = jax.random.split(jax.random.key(seed), 7)
    query_proj = gaussian(splits[0], (SEQ, WIDTH), 1.0, 6.0, ((0, 16), (1, 8)))
    key_proj = gaussian(splits[1], (SEQ, WIDTH), 1.0, 6.0, ((0, 16), (1, 8)))
    value_proj = gaussian(splits[2], (SEQ, WIDTH), 1.0, 6.0, ((0, 16), (1, 8)))
    filter_spectrum = draw_filter_spectrum(jax.random.fold_in(splits[6], 71), 0)
    skip_gain = jnp.clip(0.5 + 1.0 * jax.random.uniform(splits[4], (WIDTH,), jnp.float32) ** steps_of(splits[4], (WIDTH,), ((0, 8),), -0.2, 0.2), 0.5, 1.5)
    out_weight = noise_with(splits[5], (WIDTH, WIDTH), WIDTH ** -0.5, 0.09375, ((0, 8),), (0, 1, 8, 2.0))
    return {"query_proj": query_proj, "key_proj": key_proj, "value_proj": value_proj, "filter_spectrum": filter_spectrum, "skip_gain": skip_gain, "out_weight": out_weight}


def reference(query_proj, key_proj, value_proj, filter_spectrum, skip_gain, out_weight):
    signal = (key_proj.astype(jnp.float32) * value_proj.astype(jnp.float32)).astype(jnp.bfloat16)
    block = math.gcd(WIDTH, 256)

    def one_block(index):
        start = (index * block).astype(jnp.int32)
        piece = lax.dynamic_slice_in_dim(signal, start, block, 1).astype(jnp.float32)
        spec = lax.dynamic_slice_in_dim(filter_spectrum, start, block, 2).astype(jnp.float32)
        freq = jnp.fft.fft(piece, n=FFT_LEN, axis=0)
        product = freq * lax.complex(spec[0], spec[1])
        return jnp.real(jnp.fft.ifft(product, axis=0))[:SEQ]

    blocks = lax.map(one_block, jnp.arange(WIDTH // block, dtype=jnp.int32))
    filtered = jnp.transpose(blocks, (1, 0, 2)).reshape(SEQ, WIDTH).astype(jnp.bfloat16)
    gated = (query_proj.astype(jnp.float32) * (filtered.astype(jnp.float32) + skip_gain * signal.astype(jnp.float32))).astype(jnp.bfloat16)
    return jnp.dot(gated, out_weight, preferred_element_type=jnp.float32).astype(jnp.bfloat16)
```

```python
import functools
import math

import numpy as np

import jax
import jax.numpy as jnp
from jax import lax
from jax.experimental import pallas as pl
from jax.experimental.pallas import tpu as pltpu
from jax.sharding import PartitionSpec as P

ROWS = 256
HALF = 17
F32 = jnp.float32
BF16 = jnp.bfloat16
BIG = 56 * 1024 * 1024


def tables():
    a = np.arange(16)
    e = np.arange(HALF)
    angle = 2.0 * np.pi * np.outer(e, a) / 32.0
    first = np.concatenate([np.cos(angle), -np.sin(angle[1:16])], axis=0)
    last = np.concatenate([np.cos(angle), -np.sin(angle[1:16])], axis=0).T
    eye = np.eye(16)
    first = np.kron(first, eye)
    last = np.kron(last, eye) / 16384.0
    r = np.arange(ROWS)
    angle = 2.0 * np.pi * (np.outer(r, r) % ROWS) / ROWS
    c, s = np.cos(angle), np.sin(angle)
    forward = np.block([[c, s], [-s, c]])
    backward = np.block([[c, -s], [s, c]])
    lane = np.arange(128) // 64
    place = 256 * lane[None, :] + r[:, None]
    angle = 2.0 * np.pi * ((e[:, None, None] * place[None]) % 16384) / 16384.0
    turn = np.stack([np.cos(angle), -np.sin(angle)], axis=1)
    angle = 2.0 * np.pi * (lane[None, :] * r[:, None]) / 512.0
    side = np.stack([np.cos(angle), -np.sin(angle)])
    return first, last, forward, backward, turn, side


def shuffles():
    index = np.arange(16)
    plain = np.zeros((256, 256))
    turned = np.zeros((256, 256))
    for e in range(16):
        plain[16 * e + index, 16 * index + e] = 1.0
        turned[16 * e + 15 - index, 16 * index + e] = 1.0
    return np.stack([plain, turned])


def low_lanes(shape):
    return lax.broadcasted_iota(jnp.int32, shape, len(shape) - 1) < 64


def interleave(top, bottom):
    low = low_lanes(top.shape)
    even = jnp.where(low, top, pltpu.roll(bottom, 64, 1))
    odd = jnp.where(low, pltpu.roll(top, 64, 1), bottom)
    return even, odd


def pack_signal_kernel(key_ref, value_ref, out_ref):
    for b in range(8):
        lanes = slice(128 * b, 128 * b + 128)
        s = key_ref[:, lanes].astype(F32) * value_ref[:, lanes].astype(F32)
        even, odd = interleave(s[:ROWS], s[ROWS:])
        out_ref[2 * b] = even.astype(BF16)
        out_ref[2 * b + 1] = odd.astype(BF16)


def pack_signal(key_proj, value_proj):
    return pl.pallas_call(
        pack_signal_kernel,
        out_shape=jax.ShapeDtypeStruct((16, ROWS, 128), BF16),
        compiler_params=pltpu.CompilerParams(vmem_limit_bytes=BIG),
        name="pack_signal",
    )(key_proj, value_proj)


def pack_spectrum_kernel(shuffle_ref, spec_ref, out_ref):
    width = spec_ref.shape[2]
    rows = spec_ref[0].reshape(16, 2, 2, 16, width)
    for high in range(2):
        parts = []
        for g in range(2):
            part = rows[:, g, high].reshape(256, width)
            parts.append(jnp.dot(shuffle_ref[high], part, preferred_element_type=F32))
        if high:
            parts = parts[::-1]
        for b in range(width // 128):
            lanes = slice(128 * b, 128 * b + 128)
            even, odd = interleave(parts[0][:, lanes], parts[1][:, lanes])
            keep = slice(16 * high, 16 * high + 16)
            out_ref[2 * b, 0, keep] = even.astype(BF16).reshape(16, 16, 128)
            out_ref[2 * b + 1, 0, keep] = odd.astype(BF16).reshape(16, 16, 128)


def pack_spectrum(filter_spectrum, shuffle):
    width = 256
    return pl.pallas_call(
        pack_spectrum_kernel,
        grid=(2, 1024 // width),
        in_specs=[
            pl.BlockSpec((2, 256, 256), lambda i, j: (0, 0, 0)),
            pl.BlockSpec((1, 1024, width), lambda i, j: (i, 0, j)),
        ],
        out_specs=pl.BlockSpec((width // 64, 1, 32, 16, 128), lambda i, j: (j, i, 0, 0, 0)),
        out_shape=jax.ShapeDtypeStruct((16, 2, 32, 16, 128), BF16),
        compiler_params=pltpu.CompilerParams(vmem_limit_bytes=BIG),
        name="pack_spectrum",
    )(shuffle, filter_spectrum)


def sign_lanes(shape):
    return jnp.where(low_lanes(shape), 1.0, -1.0).astype(F32)


def forward_kernel(first_ref, turn_ref, side_ref, signal_ref, out_ref):
    sign = sign_lanes((16, 128))

    def step(q, carry):
        at = pl.ds(pl.multiple_of(16 * q, 16), 16)
        block = signal_ref[:, at, :].reshape(256, 128)
        sums = jnp.dot(first_ref[...], block, preferred_element_type=F32).reshape(32, 16, 128)
        side_re = side_ref[0, at, :]
        side_im = side_ref[1, at, :]
        for e in range(HALF):
            re = sums[e]
            cos = turn_ref[e, 0, at, :]
            sin = turn_ref[e, 1, at, :]
            if e in (0, 16):
                c_re, c_im = re * cos, re * sin
            else:
                im = sums[16 + e]
                c_re, c_im = re * cos - im * sin, re * sin + im * cos
            d_re = c_re * sign + pltpu.roll(c_re, 64, 1)
            d_im = c_im * sign + pltpu.roll(c_im, 64, 1)
            out_ref[e, 0, at, :] = (d_re * side_re - d_im * side_im).astype(BF16)
            out_ref[e, 1, at, :] = (d_re * side_im + d_im * side_re).astype(BF16)
        return carry

    lax.fori_loop(0, 16, step, 0)


def forward_part(signal, first, turn, side):
    return pl.pallas_call(
        forward_kernel,
        out_shape=jax.ShapeDtypeStruct((HALF, 2, ROWS, 128), BF16),
        compiler_params=pltpu.CompilerParams(vmem_limit_bytes=BIG),
        name="forward_part",
    )(first, turn, side, signal)


def filter_kernel(
    forward_ref, backward_ref, last_ref, turn_ref, side_ref, part_ref, spec_ref, out_ref, held
):
    sign = sign_lanes((ROWS, 128))
    side_re = side_ref[0]
    side_im = side_ref[1]

    def spectrum(which, e):
        return spec_ref[:, which, e].astype(F32).reshape(ROWS, 128)

    def mirrored(which, e):
        return jnp.concatenate([spec_ref[15 - j, which, e] for j in range(16)], axis=0).astype(F32)

    for start in range(0, HALF, 2):
        group = [e for e in (start, start + 1) if e < HALF]
        data = jnp.concatenate([part_ref[e].reshape(512, 128) for e in group], axis=1)
        x = jnp.dot(forward_ref[...], data, preferred_element_type=F32)
        products = []
        for n, e in enumerate(group):
            x_re = x[:ROWS, 128 * n : 128 * n + 128]
            x_im = x[ROWS:, 128 * n : 128 * n + 128]
            if e == 0:
                h_re, h_im = spectrum(0, 0), spectrum(1, 0)
            elif e == 16:
                h_re, h_im = mirrored(0, 16), -mirrored(1, 16)
            else:
                h_re = spectrum(0, e) + mirrored(0, 32 - e)
                h_im = spectrum(1, e) - mirrored(1, 32 - e)
            y_re = x_re * h_re - x_im * h_im
            y_im = x_re * h_im + x_im * h_re
            products.append(jnp.concatenate([y_re.astype(BF16), y_im.astype(BF16)], axis=0))
        back = jnp.dot(
            backward_ref[...], jnp.concatenate(products, axis=1), preferred_element_type=F32
        )
        for n, e in enumerate(group):
            b_re = back[:ROWS, 128 * n : 128 * n + 128]
            b_im = back[ROWS:, 128 * n : 128 * n + 128]
            s_re = b_re * side_re + b_im * side_im
            s_im = b_im * side_re - b_re * side_im
            c_re = s_re * sign + pltpu.roll(s_re, 64, 1)
            c_im = s_im * sign + pltpu.roll(s_im, 64, 1)
            cos = turn_ref[e, 0]
            sin = turn_ref[e, 1]
            held[e] = (c_re * cos + c_im * sin).astype(BF16)
            if e not in (0, 16):
                held[16 + e] = (c_im * cos - c_re * sin).astype(BF16)

    def step(q, carry):
        at = pl.ds(pl.multiple_of(16 * q, 16), 16)
        block = held[:, at, :].reshape(512, 128)
        y = jnp.dot(last_ref[...], block, preferred_element_type=F32)
        out_ref[:, at, :] = y.astype(BF16).reshape(16, 16, 128)
        return carry

    lax.fori_loop(0, 16, step, 0)


def filter_part(part, spectrum, forward, backward, last, turn, side):
    return pl.pallas_call(
        filter_kernel,
        out_shape=jax.ShapeDtypeStruct((16, ROWS, 128), BF16),
        scratch_shapes=[pltpu.VMEM((32, ROWS, 128), BF16)],
        compiler_params=pltpu.CompilerParams(vmem_limit_bytes=BIG),
        name="filter_part",
    )(forward, backward, last, turn, side, part, spectrum)


def project_kernel(query_ref, key_ref, value_ref, skip_ref, filtered_ref, weight_ref, out_ref, gated):
    @pl.when(pl.program_id(0) == 0)
    def _():
        for b in range(8):
            lanes = slice(128 * b, 128 * b + 128)
            top, bottom = interleave(
                filtered_ref[2 * b].astype(F32), filtered_ref[2 * b + 1].astype(F32)
            )
            for n, filtered in enumerate((top, bottom)):
                rows = slice(ROWS * n, ROWS * n + ROWS)
                signal = key_ref[rows, lanes].astype(F32) * value_ref[rows, lanes].astype(F32)
                signal = signal.astype(BF16).astype(F32)
                gate = filtered + skip_ref[:, lanes] * signal
                gated[rows, lanes] = (query_ref[rows, lanes].astype(F32) * gate).astype(BF16)

    out_ref[0] = jnp.dot(gated[...], weight_ref[...], preferred_element_type=F32).astype(BF16)


def project(query_proj, key_proj, value_proj, skip_gain, filtered, out_weight):
    rows, channels = query_proj.shape
    width = 1024
    blocks = out_weight.shape[1] // width
    whole = lambda i: (0, 0)
    return pl.pallas_call(
        project_kernel,
        grid=(blocks,),
        in_specs=[
            pl.BlockSpec((rows, channels), whole),
            pl.BlockSpec((rows, channels), whole),
            pl.BlockSpec((rows, channels), whole),
            pl.BlockSpec((1, channels), whole),
            pl.BlockSpec((16, ROWS, 128), lambda i: (0, 0, 0)),
            pl.BlockSpec((channels, width), lambda i: (0, i)),
        ],
        out_specs=pl.BlockSpec((1, rows, width), lambda i: (i, 0, 0)),
        out_shape=jax.ShapeDtypeStruct((blocks, rows, width), BF16),
        scratch_shapes=[pltpu.VMEM((rows, channels), BF16)],
        compiler_params=pltpu.CompilerParams(vmem_limit_bytes=BIG),
        name="project",
    )(query_proj, key_proj, value_proj, skip_gain.reshape(1, channels), filtered, out_weight)


def convolve(key_proj, value_proj, filter_spectrum):
    first, last, forward, backward, turn, side = tables()
    as_bf16 = lambda t: jnp.asarray(t.astype(np.float32)).astype(BF16)
    turn = jnp.asarray(turn.astype(np.float32))
    side = jnp.asarray(side.astype(np.float32))
    signal = pack_signal(key_proj, value_proj)
    signal = lax.all_to_all(signal, "ctx", split_axis=0, concat_axis=0, tiled=True)
    spectrum = pack_spectrum(filter_spectrum, as_bf16(shuffles()))
    spectrum = lax.all_to_all(spectrum, "ctx", split_axis=0, concat_axis=0, tiled=True)
    part = forward_part(signal, as_bf16(first), turn, side)
    out = filter_part(
        part, spectrum, as_bf16(forward), as_bf16(backward), as_bf16(last), turn, side
    )
    return lax.all_to_all(out, "ctx", split_axis=0, concat_axis=0, tiled=True)


def per_device(query_proj, key_proj, value_proj, filter_spectrum, skip_gain, out_weight):
    filtered = convolve(key_proj, value_proj, filter_spectrum)
    terms = project(query_proj, key_proj, value_proj, skip_gain, filtered, out_weight)
    out = lax.psum_scatter(terms, "tp", scatter_dimension=0, tiled=True)
    return out[0]


def solution(mesh):
    in_specs = (
        P("ctx", "tp"),
        P("ctx", "tp"),
        P("ctx", "tp"),
        P(None, "ctx", "tp"),
        P("tp"),
        P("tp", None),
    )
    out_specs = P("ctx", "tp")
    return jax.shard_map(
        per_device, mesh=mesh, in_specs=in_specs, out_specs=out_specs, check_vma=False
    )
```

```python
import functools

import numpy as np

import jax
import jax.numpy as jnp
from jax import lax
from jax.experimental import pallas as pl
from jax.experimental.pallas import tpu as pltpu
from jax.sharding import PartitionSpec as P

ROWS = 256
HALF = 17
HELD = pl.BlockSpec(memory_space=pltpu.VMEM)
FAR = pl.BlockSpec(memory_space=pltpu.HBM)
SCALARS = pl.BlockSpec(memory_space=pltpu.SMEM)
F32 = jnp.float32
BF16 = jnp.bfloat16
TIGHT = 56 * 1024 * 1024
BIG = 60 * 1024 * 1024
LITTLE = 24 * 1024 * 1024
MOST = 48 * 1024 * 1024


def tables():
    a = np.arange(16)
    e = np.arange(HALF)
    angle = 2.0 * np.pi * np.outer(e, a) / 32.0
    first = np.concatenate([np.cos(angle), -np.sin(angle[1:16])], axis=0)
    last = np.concatenate([np.cos(angle), -np.sin(angle[1:16])], axis=0).T
    eye = np.eye(16)
    first = np.kron(first, eye)
    last = np.kron(last, eye) / 16384.0
    r = np.arange(ROWS)
    angle = 2.0 * np.pi * (np.outer(r, r) % ROWS) / ROWS
    c, s = np.cos(angle), np.sin(angle)
    forward = np.block([[c, s], [-s, c]])
    backward = np.block([[c, -s], [s, c]])
    lane = np.arange(128) // 64
    place = 256 * lane[None, :] + r[:, None]
    angle = 2.0 * np.pi * ((e[:, None, None] * place[None]) % 16384) / 16384.0
    turn = np.stack([np.cos(angle), -np.sin(angle)], axis=1)
    angle = 2.0 * np.pi * (lane[None, :] * r[:, None]) / 512.0
    side = np.stack([np.cos(angle), -np.sin(angle)])
    return first, last, forward, backward, turn, side


def shuffles():
    index = np.arange(16)
    plain = np.zeros((256, 256))
    turned = np.zeros((256, 256))
    for e in range(16):
        plain[16 * e + index, 16 * index + e] = 1.0
        turned[16 * e + 15 - index, 16 * index + e] = 1.0
    return np.stack([plain, turned])


def low_lanes(shape):
    return lax.broadcasted_iota(jnp.int32, shape, len(shape) - 1) < 64


def interleave(top, bottom):
    low = low_lanes(top.shape)
    even = jnp.where(low, top, pltpu.roll(bottom, 64, 1))
    odd = jnp.where(low, pltpu.roll(top, 64, 1), bottom)
    return even, odd


def pack_signal_kernel(key_ref, value_ref, out_ref, keys, values, done):
    width = 256
    copies = []
    for n in range(4):
        lanes = pl.ds(width * n, width)
        pair = [
            pltpu.make_async_copy(source.at[:, lanes], target.at[:, lanes], done.at[m, n])
            for m, (source, target) in enumerate(((key_ref, keys), (value_ref, values)))
        ]
        for copy in pair:
            copy.start()
        copies.append(pair)
    for b in range(8):
        if b % 2 == 0:
            for copy in copies[b // 2]:
                copy.wait()
        lanes = slice(128 * b, 128 * b + 128)
        for r in range(0, ROWS, 32):
            halves = []
            for n in range(2):
                rows = slice(ROWS * n + r, ROWS * n + r + 32)
                halves.append(keys[rows, lanes].astype(F32) * values[rows, lanes].astype(F32))
            even, odd = interleave(*halves)
            out_ref[2 * b, r : r + 32] = even.astype(BF16)
            out_ref[2 * b + 1, r : r + 32] = odd.astype(BF16)


def pack_signal(key_proj, value_proj):
    return pl.pallas_call(
        pack_signal_kernel,
        in_specs=[FAR] * 2,
        out_shape=jax.ShapeDtypeStruct((16, ROWS, 128), BF16),
        scratch_shapes=[
            pltpu.VMEM(key_proj.shape, BF16),
            pltpu.VMEM(key_proj.shape, BF16),
            pltpu.SemaphoreType.DMA((2, 4)),
        ],
        compiler_params=pltpu.CompilerParams(vmem_limit_bytes=BIG),
        cost_estimate=pl.CostEstimate(flops=1 << 20, bytes_accessed=3 << 20, transcendentals=0),
        name="pack_signal",
    )(key_proj, value_proj)


def slot(e):
    if e == 16:
        return 1
    return 2 * e if e < 16 else 2 * (32 - e) + 1


def pack_spectrum_kernel(shuffle_ref, spec_ref, out_ref):
    width = 256
    for which in range(2):
        for start in range(0, spec_ref.shape[2], width):
            rows = spec_ref[which, :, start : start + width].reshape(16, 2, 2, 16, width)
            for high in range(2):
                parts = []
                for g in range(2):
                    part = rows[:, g, high].reshape(256, width)
                    parts.append(jnp.dot(shuffle_ref[high], part, preferred_element_type=F32))
                if high:
                    parts = parts[::-1]
                for b in range(width // 128):
                    lanes = slice(128 * b, 128 * b + 128)
                    even, odd = interleave(parts[0][:, lanes], parts[1][:, lanes])
                    to = start // 64 + 2 * b
                    for e in range(16):
                        keep = slice(16 * e, 16 * e + 16)
                        out_ref[to, which, slot(16 * high + e)] = even[keep].astype(BF16)
                        out_ref[to + 1, which, slot(16 * high + e)] = odd[keep].astype(BF16)


def pack_spectrum(filter_spectrum, shuffle):
    return pl.pallas_call(
        pack_spectrum_kernel,
        in_specs=[HELD] * 2,
        out_specs=HELD,
        out_shape=jax.ShapeDtypeStruct((16, 2, 32, 16, 128), BF16),
        compiler_params=pltpu.CompilerParams(vmem_limit_bytes=LITTLE),
        cost_estimate=pl.CostEstimate(flops=1 << 30, bytes_accessed=12 << 20, transcendentals=0),
        name="pack_spectrum",
    )(shuffle, filter_spectrum)


def sign_lanes(shape):
    return jnp.where(low_lanes(shape), 1.0, -1.0).astype(F32)


def forward_kernel(first_ref, forward_ref, turn_ref, side_ref, signal_ref, out_ref, part):
    sign = sign_lanes((16, 128))

    def step(q, carry):
        at = pl.ds(pl.multiple_of(16 * q, 16), 16)
        block = signal_ref[:, at, :].reshape(256, 128)
        sums = jnp.dot(first_ref[...], block, preferred_element_type=F32).reshape(32, 16, 128)
        side_re = side_ref[0, at, :]
        side_im = side_ref[1, at, :]
        for e in range(HALF):
            re = sums[e]
            cos = turn_ref[e, 0, at, :]
            sin = turn_ref[e, 1, at, :]
            if e in (0, 16):
                c_re, c_im = re * cos, re * sin
            else:
                im = sums[16 + e]
                c_re, c_im = re * cos - im * sin, re * sin + im * cos
            d_re = c_re * sign + pltpu.roll(c_re, 64, 1)
            d_im = c_im * sign + pltpu.roll(c_im, 64, 1)
            part[e, 0, at, :] = (d_re * side_re - d_im * side_im).astype(BF16)
            part[e, 1, at, :] = (d_re * side_im + d_im * side_re).astype(BF16)
        return carry

    lax.fori_loop(0, 16, step, 0)

    def pair(n, carry):
        data = jnp.concatenate(
            [part[2 * n].reshape(512, 128), part[2 * n + 1].reshape(512, 128)], axis=1
        )
        x = jnp.dot(forward_ref[...], data, preferred_element_type=F32).astype(BF16)
        out_ref[2 * n] = x[:, :128].reshape(2, ROWS, 128)
        out_ref[2 * n + 1] = x[:, 128:].reshape(2, ROWS, 128)
        return carry

    lax.fori_loop(0, 8, pair, 0)
    x = jnp.dot(forward_ref[...], part[16].reshape(512, 128), preferred_element_type=F32)
    out_ref[16] = x.astype(BF16).reshape(2, ROWS, 128)


def forward_part(signal, first, forward, turn, side):
    return pl.pallas_call(
        forward_kernel,
        in_specs=[HELD] * 5,
        out_specs=HELD,
        out_shape=jax.ShapeDtypeStruct((HALF, 2, ROWS, 128), BF16),
        scratch_shapes=[pltpu.VMEM((HALF, 2, ROWS, 128), BF16)],
        compiler_params=pltpu.CompilerParams(vmem_limit_bytes=MOST),
        cost_estimate=pl.CostEstimate(flops=2 << 30, bytes_accessed=12 << 20, transcendentals=0),
        name="forward_part",
    )(first, forward, turn, side, signal)


def filter_kernel(
    backward_from,
    last_from,
    side_from,
    turn_from,
    x_ref,
    spec_ref,
    out_ref,
    backward_ref,
    last_ref,
    side_ref,
    turn_ref,
    held,
    products,
    sums,
    table_done,
    turn_done,
):
    tables = [
        pltpu.make_async_copy(source, target, table_done.at[n])
        for n, (source, target) in enumerate(
            ((backward_from, backward_ref), (side_from, side_ref), (last_from, last_ref))
        )
    ]
    turns = []
    for g in range(9):
        some = pl.ds(2 * g, 2 if g < 8 else 1)
        turns.append(
            pltpu.make_async_copy(turn_from.at[some], turn_ref.at[some], turn_done.at[g])
        )
    for copy in tables[:2] + turns + tables[2:]:
        copy.start()
    sign = sign_lanes((16, 128))

    def spectrum(j, which, place):
        return spec_ref[j, which, place].astype(F32)

    def filter_at(e, j):
        if e == 0:
            return spectrum(j, 0, 0), spectrum(j, 1, 0)
        if e == 16:
            return spectrum(15 - j, 0, 1), -spectrum(15 - j, 1, 1)
        h_re = spectrum(j, 0, 2 * e) + spectrum(15 - j, 0, 2 * e + 1)
        h_im = spectrum(j, 1, 2 * e) - spectrum(15 - j, 1, 2 * e + 1)
        return h_re, h_im

    for start in range(0, HALF, 2):
        group = range(start, min(start + 2, HALF))
        for n, e in enumerate(group):
            lanes = slice(128 * n, 128 * n + 128)
            for j in range(16):
                rows = slice(16 * j, 16 * j + 16)
                below = slice(ROWS + 16 * j, ROWS + 16 * j + 16)
                h_re, h_im = filter_at(e, j)
                x_re, x_im = x_ref[e, 0, rows].astype(F32), x_ref[e, 1, rows].astype(F32)
                products[start // 2, rows, lanes] = (x_re * h_re - x_im * h_im).astype(BF16)
                products[start // 2, below, lanes] = (x_re * h_im + x_im * h_re).astype(BF16)
        wide = 128 * len(group)
        if start == 0:
            tables[0].wait()
        sums[start // 2, :, :wide] = jnp.dot(
            backward_ref[...], products[start // 2, :, :wide], preferred_element_type=F32
        )
        if start == 0:
            tables[1].wait()
        turns[start // 2].wait()
        for n, e in enumerate(group):
            lanes = slice(128 * n, 128 * n + 128)
            for j in range(16):
                rows = slice(16 * j, 16 * j + 16)
                below = slice(ROWS + 16 * j, ROWS + 16 * j + 16)
                b_re = sums[start // 2, rows, lanes]
                b_im = sums[start // 2, below, lanes]
                side_re, side_im = side_ref[0, rows], side_ref[1, rows]
                s_re = b_re * side_re + b_im * side_im
                s_im = b_im * side_re - b_re * side_im
                c_re = s_re * sign + pltpu.roll(s_re, 64, 1)
                c_im = s_im * sign + pltpu.roll(s_im, 64, 1)
                cos, sin = turn_ref[e, 0, rows], turn_ref[e, 1, rows]
                held[e, rows] = (c_re * cos + c_im * sin).astype(BF16)
                if e not in (0, 16):
                    held[16 + e, rows] = (c_im * cos - c_re * sin).astype(BF16)

    tables[2].wait()
    for q in range(0, 16, 2):
        block = jnp.concatenate(
            [held[:, 16 * p : 16 * p + 16].reshape(512, 128) for p in (q, q + 1)], axis=1
        )
        y = jnp.dot(last_ref[...], block, preferred_element_type=F32).astype(BF16)
        for n in range(2):
            out_ref[:, 16 * (q + n) : 16 * (q + n) + 16] = y[:, 128 * n : 128 * n + 128].reshape(
                16, 16, 128
            )


def filter_part(x, spectrum, backward, last, turn, side):
    return pl.pallas_call(
        filter_kernel,
        in_specs=[FAR] * 4 + [HELD] * 2,
        out_specs=HELD,
        out_shape=jax.ShapeDtypeStruct((16, ROWS, 128), BF16),
        scratch_shapes=[
            *[pltpu.VMEM(t.shape, t.dtype) for t in (backward, last, side, turn)],
            pltpu.VMEM((32, ROWS, 128), BF16),
            pltpu.VMEM((9, 2 * ROWS, 256), BF16),
            pltpu.VMEM((9, 2 * ROWS, 256), F32),
            pltpu.SemaphoreType.DMA((3,)),
            pltpu.SemaphoreType.DMA((9,)),
        ],
        compiler_params=pltpu.CompilerParams(vmem_limit_bytes=TIGHT),
        cost_estimate=pl.CostEstimate(flops=2 << 30, bytes_accessed=16 << 20, transcendentals=0),
        name="filter_part",
    )(backward, last, side, turn, x, spectrum)


def gate_kernel(query_ref, key_ref, value_ref, skip_ref, filtered_ref, out_ref):
    for b in range(query_ref.shape[1] // 128):
        lanes = slice(128 * b, 128 * b + 128)
        skip = skip_ref[:, lanes]
        for r in range(0, ROWS, 32):
            halves = interleave(
                filtered_ref[2 * b, r : r + 32].astype(F32),
                filtered_ref[2 * b + 1, r : r + 32].astype(F32),
            )
            for n, filtered in enumerate(halves):
                rows = slice(ROWS * n + r, ROWS * n + r + 32)
                signal = key_ref[rows, lanes].astype(F32) * value_ref[rows, lanes].astype(F32)
                signal = signal.astype(BF16).astype(F32)
                held = filtered + skip * signal
                out_ref[rows, lanes] = (query_ref[rows, lanes].astype(F32) * held).astype(BF16)


def gate(query_proj, key_proj, value_proj, skip_gain, filtered):
    rows, channels = query_proj.shape
    return pl.pallas_call(
        gate_kernel,
        in_specs=[HELD] * 5,
        out_specs=HELD,
        out_shape=jax.ShapeDtypeStruct((rows, channels), BF16),
        compiler_params=pltpu.CompilerParams(vmem_limit_bytes=LITTLE),
        cost_estimate=pl.CostEstimate(flops=4 << 20, bytes_accessed=5 << 20, transcendentals=0),
        name="gate",
    )(query_proj, key_proj, value_proj, skip_gain.reshape(1, channels), filtered)


def far_kernel(own_ref, other_ref, weight_ref, other_weight_ref, top_ref, bottom_ref):
    width = 256
    for start in range(0, weight_ref.shape[1], width):
        lanes = slice(start, start + width)
        total = jnp.dot(own_ref[...], weight_ref[:, lanes], preferred_element_type=F32)
        total += jnp.dot(other_ref[...], other_weight_ref[:, lanes], preferred_element_type=F32)
        top_ref[:, lanes] = total[:ROWS].astype(BF16)
        bottom_ref[:, lanes] = total[ROWS:].astype(BF16)


def far_product(own, other, weight, other_weight):
    shape = jax.ShapeDtypeStruct((ROWS, weight.shape[1]), BF16)
    return pl.pallas_call(
        far_kernel,
        in_specs=[HELD] * 4,
        out_specs=[HELD] * 2,
        out_shape=[shape, shape],
        compiler_params=pltpu.CompilerParams(vmem_limit_bytes=LITTLE),
        cost_estimate=pl.CostEstimate(flops=2 << 30, bytes_accessed=6 << 20, transcendentals=0),
        name="far_product",
    )(own, other, weight, other_weight)


def near_kernel(flip, place_ref, own_ref, other_ref, weight_ref, other_weight_ref, *refs):
    outs, (held, done) = refs[:2], refs[2:]
    columns = outs[0].shape[1]
    width = columns // 2
    steps = [(b, i) for b in range(2) for i in range(2)]
    arrivals = []
    for b, i in steps:
        at = pl.ds(pl.multiple_of(place_ref[b] * columns + width * i, width), width)
        arrivals.append(
            [
                pltpu.make_async_copy(w.at[:, at], held.at[b, i, m], done.at[b, i, m])
                for m, w in enumerate((weight_ref, other_weight_ref))
            ]
        )
    for copy in sum(arrivals, []):
        copy.start()
    for (b, i), pair in zip(steps, arrivals):
        for copy in pair:
            copy.wait()
        rows = slice(ROWS, 2 * ROWS) if (b == 0) == flip else slice(0, ROWS)
        total = jnp.dot(own_ref[rows], held[b, i, 0], preferred_element_type=F32)
        total += jnp.dot(other_ref[rows], held[b, i, 1], preferred_element_type=F32)
        outs[b][:, width * i : width * i + width] = total.astype(BF16)


def near_product(own, other, out_weight, other_weight, blocks, flip):
    channels = own.shape[1]
    columns = out_weight.shape[1] // 8
    return pl.pallas_call(
        functools.partial(near_kernel, flip),
        in_specs=[SCALARS] + [HELD] * 2 + [FAR] * 2,
        out_specs=[HELD] * 2,
        out_shape=[jax.ShapeDtypeStruct((ROWS, columns), BF16)] * 2,
        scratch_shapes=[
            pltpu.VMEM((2, 2, 2, channels, columns // 2), BF16),
            pltpu.SemaphoreType.DMA((2, 2, 2)),
        ],
        compiler_params=pltpu.CompilerParams(vmem_limit_bytes=MOST),
        cost_estimate=pl.CostEstimate(flops=2 << 30, bytes_accessed=10 << 20, transcendentals=0),
        name="near_product",
    )(blocks, own, other, out_weight, other_weight)


def own_kernel(
    place_ref,
    own_ref,
    other_ref,
    weight_ref,
    other_weight_ref,
    top_more_ref,
    bottom_more_ref,
    top_ref,
    bottom_ref,
):
    total = jnp.dot(own_ref[...], weight_ref[...], preferred_element_type=F32)
    total += jnp.dot(other_ref[...], other_weight_ref[...], preferred_element_type=F32)
    top_ref[...] = total[:ROWS] + top_more_ref[...].astype(F32)
    bottom_ref[...] = total[ROWS:] + bottom_more_ref[...].astype(F32)


def own_product(own, other, out_weight, other_weight, block, top_more, bottom_more):
    rows, channels = own.shape
    columns = out_weight.shape[1] // 8
    width = 512
    steps = columns // width
    data = pl.BlockSpec((rows, channels), lambda i, at: (0, 0))
    weight = pl.BlockSpec((channels, width), lambda i, at: (0, at[0] * steps + i))
    half = pl.BlockSpec((ROWS, width), lambda i, at: (0, i))
    shape = jax.ShapeDtypeStruct((ROWS, columns), F32)
    return pl.pallas_call(
        own_kernel,
        grid_spec=pltpu.PrefetchScalarGridSpec(
            num_scalar_prefetch=1,
            grid=(steps,),
            in_specs=[data, data, weight, weight, half, half],
            out_specs=[half, half],
        ),
        out_shape=[shape, shape],
        compiler_params=pltpu.CompilerParams(vmem_limit_bytes=MOST),
        cost_estimate=pl.CostEstimate(flops=2 << 30, bytes_accessed=10 << 20, transcendentals=0),
        name="own_product",
    )(block, own, other, out_weight, other_weight, top_more, bottom_more)


def finish_kernel(top_ref, bottom_ref, top_more_ref, bottom_more_ref, out_ref):
    out_ref[:ROWS] = (top_ref[...] + top_more_ref[...].astype(F32)).astype(BF16)
    out_ref[ROWS:] = (bottom_ref[...] + bottom_more_ref[...].astype(F32)).astype(BF16)


def finish(top, bottom, top_more, bottom_more):
    columns = top.shape[1]
    width = 512
    half = pl.BlockSpec((ROWS, width), lambda i: (0, i))
    return pl.pallas_call(
        finish_kernel,
        grid=(columns // width,),
        in_specs=[half] * 4,
        out_specs=pl.BlockSpec((2 * ROWS, width), lambda i: (0, i)),
        out_shape=jax.ShapeDtypeStruct((2 * ROWS, columns), BF16),
        compiler_params=pltpu.CompilerParams(vmem_limit_bytes=MOST),
        name="finish",
    )(top, bottom, top_more, bottom_more)


def chip_shift(array, step):
    return lax.ppermute(array, "tp", [(i, (i + 2 * step) % 8) for i in range(8)])


def core_swap(array):
    return lax.ppermute(array, "tp", [(i, i ^ 1) for i in range(8)])


def block_of(step):
    place = lax.axis_index("tp")
    return 2 * ((place // 2 + step) % 4) + place % 2


def far_weights(out_weight, other_weight):
    width = out_weight.shape[1] // 8
    start = block_of(2) * width
    return [lax.dynamic_slice_in_dim(w, start, width, 1) for w in (out_weight, other_weight)]


def project(gated, out_weight, other_weight, far):
    other = core_swap(gated)
    add = lambda a, b: (a.astype(F32) + b.astype(F32)).astype(BF16)
    far_top, far_bottom = far_product(gated, other, *far)
    up = chip_shift(far_top, 1)
    down = chip_shift(far_bottom, -1)
    near = jnp.stack([block_of(1), block_of(3)])
    next_bottom, last_top = near_product(gated, other, out_weight, other_weight, near, True)
    up_direct = chip_shift(next_bottom, 1)
    down_direct = chip_shift(last_top, -1)
    next_top, last_bottom = near_product(gated, other, out_weight, other_weight, near, False)
    up_sum = chip_shift(add(next_top, up), 1)
    down_sum = chip_shift(add(last_bottom, down), -1)
    top, bottom = own_product(
        gated, other, out_weight, other_weight, block_of(0).reshape(1), down_direct, up_direct
    )
    return finish(top, bottom, up_sum, down_sum)


def convolve(key_proj, value_proj, filter_spectrum, early=()):
    first, last, forward, backward, turn, side = tables()
    as_bf16 = lambda t: jnp.asarray(t.astype(np.float32)).astype(BF16)
    turn = jnp.asarray(turn.astype(np.float32))
    side = jnp.asarray(side.astype(np.float32))
    signal = pack_signal(key_proj, value_proj)
    signal = lax.all_to_all(signal, "ctx", split_axis=0, concat_axis=0, tiled=True)
    spectrum = pack_spectrum(filter_spectrum, as_bf16(shuffles()))
    signal, spectrum = lax.optimization_barrier((signal, spectrum))
    spectrum = lax.all_to_all(spectrum, "ctx", split_axis=0, concat_axis=0, tiled=True)
    x = forward_part(signal, as_bf16(first), as_bf16(forward), turn, side)
    x, *early = lax.optimization_barrier((x, *early))
    out = filter_part(x, spectrum, as_bf16(backward), as_bf16(last), turn, side)
    return lax.all_to_all(out, "ctx", split_axis=0, concat_axis=0, tiled=True), early


def per_device(query_proj, key_proj, value_proj, filter_spectrum, skip_gain, out_weight):
    other_weight = core_swap(out_weight)
    far = far_weights(out_weight, other_weight)
    filtered, far = convolve(key_proj, value_proj, filter_spectrum, far)
    gated = gate(query_proj, key_proj, value_proj, skip_gain, filtered)
    return project(gated, out_weight, other_weight, far)


def solution(mesh):
    in_specs = (
        P("ctx", "tp"),
        P("ctx", "tp"),
        P("ctx", "tp"),
        P(None, "ctx", "tp"),
        P("tp"),
        P("tp", None),
    )
    out_specs = P("ctx", "tp")
    return jax.shard_map(
        per_device, mesh=mesh, in_specs=in_specs, out_specs=out_specs, check_vma=False
    )
```

```python
import functools
import math

import numpy as np

import jax
import jax.numpy as jnp
from jax import lax
from jax.experimental import pallas as pl
from jax.experimental.pallas import tpu as pltpu
from jax.sharding import PartitionSpec as P

ROWS = 256
HALF = 17
HELD = pl.BlockSpec(memory_space=pltpu.VMEM)
FAR = pl.BlockSpec(memory_space=pltpu.HBM)
SCALARS = pl.BlockSpec(memory_space=pltpu.SMEM)
F32 = jnp.float32
BF16 = jnp.bfloat16
TIGHT = 46 * 1024 * 1024
BIG = 60 * 1024 * 1024
LITTLE = 24 * 1024 * 1024
MOST = 48 * 1024 * 1024


def tables():
    a = np.arange(16)
    e = np.arange(HALF)
    angle = 2.0 * np.pi * np.outer(e, a) / 32.0
    first = np.concatenate([np.cos(angle), -np.sin(angle[1:16])], axis=0)
    last = np.concatenate([np.cos(angle), -np.sin(angle[1:16])], axis=0).T
    eye = np.eye(16)
    first = np.kron(first, eye)
    last = np.kron(last, eye) / 16384.0
    r = np.arange(ROWS)
    angle = 2.0 * np.pi * (np.outer(r, r) % ROWS) / ROWS
    c, s = np.cos(angle), np.sin(angle)
    forward = np.block([[c, s], [-s, c]])
    backward = np.block([[c, -s], [s, c]])
    lane = np.arange(128) // 64
    place = 256 * lane[None, :] + r[:, None]
    angle = 2.0 * np.pi * ((e[:, None, None] * place[None]) % 16384) / 16384.0
    turn = np.stack([np.cos(angle), -np.sin(angle)], axis=1)
    angle = 2.0 * np.pi * (lane[None, :] * r[:, None]) / 512.0
    side = np.stack([np.cos(angle), -np.sin(angle)])
    return first, last, forward, backward, turn, side


def shuffles():
    index = np.arange(16)
    plain = np.zeros((256, 256))
    turned = np.zeros((256, 256))
    for e in range(16):
        plain[16 * e + index, 16 * index + e] = 1.0
        turned[16 * e + 15 - index, 16 * index + e] = 1.0
    return np.stack([plain, turned])


def low_lanes(shape):
    return lax.broadcasted_iota(jnp.int32, shape, len(shape) - 1) < 64


def interleave(top, bottom):
    low = low_lanes(top.shape)
    even = jnp.where(low, top, pltpu.roll(bottom, 64, 1))
    odd = jnp.where(low, pltpu.roll(top, 64, 1), bottom)
    return even, odd


def pack_signal_kernel(key_ref, value_ref, out_ref, keys, values, done):
    width = 256
    copies = []
    for n in range(4):
        lanes = pl.ds(width * n, width)
        pair = [
            pltpu.make_async_copy(source.at[:, lanes], target.at[:, lanes], done.at[m, n])
            for m, (source, target) in enumerate(((key_ref, keys), (value_ref, values)))
        ]
        for copy in pair:
            copy.start()
        copies.append(pair)
    for b in range(8):
        if b % 2 == 0:
            for copy in copies[b // 2]:
                copy.wait()
        lanes = slice(128 * b, 128 * b + 128)
        for r in range(0, ROWS, 32):
            halves = []
            for n in range(2):
                rows = slice(ROWS * n + r, ROWS * n + r + 32)
                halves.append(keys[rows, lanes].astype(F32) * values[rows, lanes].astype(F32))
            even, odd = interleave(*halves)
            out_ref[2 * b, r : r + 32] = even.astype(BF16)
            out_ref[2 * b + 1, r : r + 32] = odd.astype(BF16)


def pack_signal(key_proj, value_proj):
    return pl.pallas_call(
        pack_signal_kernel,
        in_specs=[FAR] * 2,
        out_specs=HELD,
        out_shape=jax.ShapeDtypeStruct((16, ROWS, 128), BF16),
        scratch_shapes=[
            pltpu.VMEM(key_proj.shape, BF16),
            pltpu.VMEM(key_proj.shape, BF16),
            pltpu.SemaphoreType.DMA((2, 4)),
        ],
        compiler_params=pltpu.CompilerParams(vmem_limit_bytes=BIG),
        cost_estimate=pl.CostEstimate(flops=1 << 20, bytes_accessed=3 << 20, transcendentals=0),
        name="pack_signal",
    )(key_proj, value_proj)


def slot(e):
    if e == 16:
        return 1
    return 2 * e if e < 16 else 2 * (32 - e) + 1


def pack_spectrum_kernel(shuffle_ref, spec_ref, out_ref):
    width = 256
    for which in range(2):
        for start in range(0, spec_ref.shape[2], width):
            rows = spec_ref[which, :, start : start + width].reshape(16, 2, 2, 16, width)
            for high in range(2):
                parts = []
                for g in range(2):
                    part = rows[:, g, high].reshape(256, width)
                    parts.append(jnp.dot(shuffle_ref[high], part, preferred_element_type=F32))
                if high:
                    parts = parts[::-1]
                for b in range(width // 128):
                    lanes = slice(128 * b, 128 * b + 128)
                    even, odd = interleave(parts[0][:, lanes], parts[1][:, lanes])
                    to = start // 64 + 2 * b
                    for e in range(16):
                        keep = slice(16 * e, 16 * e + 16)
                        out_ref[to, which, slot(16 * high + e)] = even[keep].astype(BF16)
                        out_ref[to + 1, which, slot(16 * high + e)] = odd[keep].astype(BF16)


def pack_spectrum(filter_spectrum, shuffle):
    return pl.pallas_call(
        pack_spectrum_kernel,
        in_specs=[HELD] * 2,
        out_specs=HELD,
        out_shape=jax.ShapeDtypeStruct((16, 2, 32, 16, 128), BF16),
        compiler_params=pltpu.CompilerParams(vmem_limit_bytes=LITTLE),
        cost_estimate=pl.CostEstimate(flops=1 << 30, bytes_accessed=12 << 20, transcendentals=0),
        name="pack_spectrum",
    )(shuffle, filter_spectrum)


def sign_lanes(shape):
    return jnp.where(low_lanes(shape), 1.0, -1.0).astype(F32)


def forward_kernel(first_ref, forward_ref, turn_ref, signal_ref, out_ref, part):
    side_ref = turn_ref.at[HALF]
    sign = sign_lanes((16, 128))

    def step(q, carry):
        at = pl.ds(pl.multiple_of(16 * q, 16), 16)
        block = signal_ref[:, at, :].reshape(256, 128)
        sums = jnp.dot(first_ref[...], block, preferred_element_type=F32).reshape(32, 16, 128)
        side_re = side_ref[0, at, :]
        side_im = side_ref[1, at, :]
        for e in range(HALF):
            re = sums[e]
            cos = turn_ref[e, 0, at, :]
            sin = turn_ref[e, 1, at, :]
            if e in (0, 16):
                c_re, c_im = re * cos, re * sin
            else:
                im = sums[16 + e]
                c_re, c_im = re * cos - im * sin, re * sin + im * cos
            d_re = c_re * sign + pltpu.roll(c_re, 64, 1)
            d_im = c_im * sign + pltpu.roll(c_im, 64, 1)
            part[e, 0, at, :] = (d_re * side_re - d_im * side_im).astype(BF16)
            part[e, 1, at, :] = (d_re * side_im + d_im * side_re).astype(BF16)
        return carry

    lax.fori_loop(0, 16, step, 0)

    def pair(n, carry):
        data = jnp.concatenate(
            [part[2 * n].reshape(512, 128), part[2 * n + 1].reshape(512, 128)], axis=1
        )
        x = jnp.dot(forward_ref[...], data, preferred_element_type=F32).astype(BF16)
        out_ref[2 * n] = x[:, :128].reshape(2, ROWS, 128)
        out_ref[2 * n + 1] = x[:, 128:].reshape(2, ROWS, 128)
        return carry

    lax.fori_loop(0, 8, pair, 0)
    x = jnp.dot(forward_ref[...], part[16].reshape(512, 128), preferred_element_type=F32)
    out_ref[16] = x.astype(BF16).reshape(2, ROWS, 128)


def forward_part(signal, first, forward, turn):
    return pl.pallas_call(
        forward_kernel,
        in_specs=[HELD] * 4,
        out_specs=HELD,
        out_shape=jax.ShapeDtypeStruct((HALF, 2, ROWS, 128), BF16),
        scratch_shapes=[pltpu.VMEM((HALF, 2, ROWS, 128), BF16)],
        compiler_params=pltpu.CompilerParams(vmem_limit_bytes=MOST),
        cost_estimate=pl.CostEstimate(flops=2 << 30, bytes_accessed=12 << 20, transcendentals=0),
        name="forward_part",
    )(first, forward, turn, signal)


def filter_kernel(
    tables_from,
    waves_from,
    x_ref,
    spec_ref,
    out_ref,
    tables_ref,
    waves_ref,
    held,
    products,
    sums,
    table_done,
):
    backward_ref = tables_ref.at[: 2 * ROWS]
    last_ref = tables_ref.at[2 * ROWS :]
    copies = [
        pltpu.make_async_copy(source.at[some], target.at[some], table_done.at[n])
        for n, (source, target, some) in enumerate(
            (
                (tables_from, tables_ref, pl.ds(0, 2 * ROWS)),
                (waves_from, waves_ref, pl.ds(0, HALF + 16)),
                (tables_from, tables_ref, pl.ds(2 * ROWS, ROWS)),
            )
        )
    ]
    for copy in copies:
        copy.start()
    sign = sign_lanes((16, 128))

    def spectrum(j, which, place):
        return spec_ref[j, which, place].astype(F32)

    def filter_at(e, j):
        if e == 0:
            return spectrum(j, 0, 0), spectrum(j, 1, 0)
        if e == 16:
            return spectrum(15 - j, 0, 1), -spectrum(15 - j, 1, 1)
        h_re = spectrum(j, 0, 2 * e) + spectrum(15 - j, 0, 2 * e + 1)
        h_im = spectrum(j, 1, 2 * e) - spectrum(15 - j, 1, 2 * e + 1)
        return h_re, h_im

    for start in range(0, HALF, 2):
        group = range(start, min(start + 2, HALF))
        for n, e in enumerate(group):
            lanes = slice(128 * n, 128 * n + 128)
            for j in range(16):
                rows = slice(16 * j, 16 * j + 16)
                below = slice(ROWS + 16 * j, ROWS + 16 * j + 16)
                h_re, h_im = filter_at(e, j)
                x_re, x_im = x_ref[e, 0, rows].astype(F32), x_ref[e, 1, rows].astype(F32)
                products[start // 2, rows, lanes] = (x_re * h_re - x_im * h_im).astype(BF16)
                products[start // 2, below, lanes] = (x_re * h_im + x_im * h_re).astype(BF16)
        wide = 128 * len(group)
        if start == 0:
            copies[0].wait()
        sums[start // 2, :, :wide] = jnp.dot(
            backward_ref[...], products[start // 2, :, :wide], preferred_element_type=F32
        )
        if start == 0:
            copies[1].wait()
        for n, e in enumerate(group):
            base_re, base_im = waves_ref[e, 0], waves_ref[e, 1]
            lanes = slice(128 * n, 128 * n + 128)
            for j in range(16):
                rows = slice(16 * j, 16 * j + 16)
                below = slice(ROWS + 16 * j, ROWS + 16 * j + 16)
                b_re = sums[start // 2, rows, lanes]
                b_im = sums[start // 2, below, lanes]
                side_re, side_im = waves_ref[HALF + j, 0], waves_ref[HALF + j, 1]
                s_re = b_re * side_re + b_im * side_im
                s_im = b_im * side_re - b_re * side_im
                c_re = s_re * sign + pltpu.roll(s_re, 64, 1)
                c_im = s_im * sign + pltpu.roll(s_im, 64, 1)
                angle = 2.0 * math.pi * (16 * j * e % 16384) / 16384.0
                step_re, step_im = math.cos(angle), -math.sin(angle)
                cos = base_re * step_re - base_im * step_im
                sin = base_re * step_im + base_im * step_re
                held[e, rows] = (c_re * cos + c_im * sin).astype(BF16)
                if e not in (0, 16):
                    held[16 + e, rows] = (c_im * cos - c_re * sin).astype(BF16)

    copies[2].wait()
    for q in range(0, 16, 2):
        block = jnp.concatenate(
            [held[:, 16 * p : 16 * p + 16].reshape(512, 128) for p in (q, q + 1)], axis=1
        )
        y = jnp.dot(last_ref[...], block, preferred_element_type=F32).astype(BF16)
        for n in range(2):
            out_ref[:, 16 * (q + n) : 16 * (q + n) + 16] = y[:, 128 * n : 128 * n + 128].reshape(
                16, 16, 128
            )


def filter_part(x, spectrum, tables, waves):
    return pl.pallas_call(
        filter_kernel,
        in_specs=[FAR] * 2 + [HELD] * 2,
        out_specs=HELD,
        out_shape=jax.ShapeDtypeStruct((16, ROWS, 128), BF16),
        scratch_shapes=[
            *[pltpu.VMEM(t.shape, t.dtype) for t in (tables, waves)],
            pltpu.VMEM((32, ROWS, 128), BF16),
            pltpu.VMEM((9, 2 * ROWS, 256), BF16),
            pltpu.VMEM((9, 2 * ROWS, 256), F32),
            pltpu.SemaphoreType.DMA((3,)),
        ],
        compiler_params=pltpu.CompilerParams(vmem_limit_bytes=TIGHT),
        cost_estimate=pl.CostEstimate(flops=2 << 30, bytes_accessed=16 << 20, transcendentals=0),
        name="filter_part",
    )(tables, waves, x, spectrum)


def gate_kernel(query_ref, key_ref, value_ref, skip_ref, filtered_ref, out_ref):
    for b in range(query_ref.shape[1] // 128):
        lanes = slice(128 * b, 128 * b + 128)
        skip = skip_ref[:, lanes]
        for r in range(0, ROWS, 32):
            halves = interleave(
                filtered_ref[2 * b, r : r + 32].astype(F32),
                filtered_ref[2 * b + 1, r : r + 32].astype(F32),
            )
            for n, filtered in enumerate(halves):
                rows = slice(ROWS * n + r, ROWS * n + r + 32)
                signal = key_ref[rows, lanes].astype(F32) * value_ref[rows, lanes].astype(F32)
                signal = signal.astype(BF16).astype(F32)
                held = filtered + skip * signal
                out_ref[rows, lanes] = (query_ref[rows, lanes].astype(F32) * held).astype(BF16)


def gate(query_proj, key_proj, value_proj, skip_gain, filtered):
    rows, channels = query_proj.shape
    return pl.pallas_call(
        gate_kernel,
        in_specs=[HELD] * 5,
        out_specs=HELD,
        out_shape=jax.ShapeDtypeStruct((rows, channels), BF16),
        compiler_params=pltpu.CompilerParams(vmem_limit_bytes=LITTLE),
        cost_estimate=pl.CostEstimate(flops=4 << 20, bytes_accessed=5 << 20, transcendentals=0),
        name="gate",
    )(query_proj, key_proj, value_proj, skip_gain.reshape(1, channels), filtered)


def far_own_kernel(own_ref, weight_ref, out_ref):
    out_ref[...] = jnp.dot(own_ref[...], weight_ref[...], preferred_element_type=F32)


def far_kernel(own_ref, other_ref, weight_ref, top_ref, bottom_ref):
    width = 256
    for start in range(0, weight_ref.shape[1], width):
        lanes = slice(start, start + width)
        total = own_ref[:, lanes]
        total += jnp.dot(other_ref[...], weight_ref[:, lanes], preferred_element_type=F32)
        top_ref[:, lanes] = total[:ROWS].astype(BF16)
        bottom_ref[:, lanes] = total[ROWS:].astype(BF16)


def far_own_product(own, weight):
    return pl.pallas_call(
        far_own_kernel,
        in_specs=[HELD] * 2,
        out_specs=HELD,
        out_shape=jax.ShapeDtypeStruct((own.shape[0], weight.shape[1]), F32),
        compiler_params=pltpu.CompilerParams(vmem_limit_bytes=LITTLE),
        cost_estimate=pl.CostEstimate(flops=1 << 30, bytes_accessed=5 << 20, transcendentals=0),
        name="far_own_product",
    )(own, weight)


def far_product(own, other, weight):
    shape = jax.ShapeDtypeStruct((ROWS, weight.shape[1]), BF16)
    return pl.pallas_call(
        far_kernel,
        in_specs=[HELD] * 3,
        out_specs=[HELD] * 2,
        out_shape=[shape, shape],
        compiler_params=pltpu.CompilerParams(vmem_limit_bytes=LITTLE),
        cost_estimate=pl.CostEstimate(flops=1 << 30, bytes_accessed=5 << 20, transcendentals=0),
        name="far_product",
    )(own, other, weight)


def near_kernel(place_ref, own_ref, other_ref, weight_ref, other_weight_ref, *refs):
    outs, (held, done) = refs[:4], refs[4:]
    columns = outs[0].shape[1]
    width = columns // 2
    steps = [(b, i) for b in range(2) for i in range(2)]
    arrivals = []
    for b, i in steps:
        at = pl.ds(pl.multiple_of(place_ref[b] * columns + width * i, width), width)
        arrivals.append(
            [
                pltpu.make_async_copy(w.at[:, at], held.at[b, i, m], done.at[b, i, m])
                for m, w in enumerate((weight_ref, other_weight_ref))
            ]
        )
    for copy in sum(arrivals, []):
        copy.start()
    for (b, i), pair in zip(steps, arrivals):
        for copy in pair:
            copy.wait()
        lanes = slice(width * i, width * i + width)
        total = jnp.dot(own_ref[...], held[b, i, 0], preferred_element_type=F32)
        total += jnp.dot(other_ref[...], held[b, i, 1], preferred_element_type=F32)
        outs[2 * b][:, lanes] = total[:ROWS].astype(BF16)
        outs[2 * b + 1][:, lanes] = total[ROWS:].astype(BF16)


def near_product(own, other, out_weight, other_weight, blocks):
    channels = own.shape[1]
    columns = out_weight.shape[1] // 8
    return pl.pallas_call(
        near_kernel,
        in_specs=[SCALARS] + [HELD] * 2 + [FAR] * 2,
        out_specs=[HELD] * 4,
        out_shape=[jax.ShapeDtypeStruct((ROWS, columns), BF16)] * 4,
        scratch_shapes=[
            pltpu.VMEM((2, 2, 2, channels, columns // 2), BF16),
            pltpu.SemaphoreType.DMA((2, 2, 2)),
        ],
        compiler_params=pltpu.CompilerParams(vmem_limit_bytes=MOST),
        cost_estimate=pl.CostEstimate(flops=4 << 30, bytes_accessed=10 << 20, transcendentals=0),
        name="near_product",
    )(blocks, own, other, out_weight, other_weight)


def own_kernel(
    place_ref,
    own_ref,
    other_ref,
    weight_ref,
    other_weight_ref,
    top_more_ref,
    bottom_more_ref,
    top_ref,
    bottom_ref,
):
    total = jnp.dot(own_ref[...], weight_ref[...], preferred_element_type=F32)
    total += jnp.dot(other_ref[...], other_weight_ref[...], preferred_element_type=F32)
    top_ref[...] = total[:ROWS] + top_more_ref[...].astype(F32)
    bottom_ref[...] = total[ROWS:] + bottom_more_ref[...].astype(F32)


def own_product(own, other, out_weight, other_weight, block, top_more, bottom_more):
    rows, channels = own.shape
    columns = out_weight.shape[1] // 8
    width = 512
    steps = columns // width
    data = pl.BlockSpec((rows, channels), lambda i, at: (0, 0))
    weight = pl.BlockSpec((channels, width), lambda i, at: (0, at[0] * steps + i))
    half = pl.BlockSpec((ROWS, width), lambda i, at: (0, i))
    shape = jax.ShapeDtypeStruct((ROWS, columns), F32)
    return pl.pallas_call(
        own_kernel,
        grid_spec=pltpu.PrefetchScalarGridSpec(
            num_scalar_prefetch=1,
            grid=(steps,),
            in_specs=[data, data, weight, weight, half, half],
            out_specs=[half, half],
        ),
        out_shape=[shape, shape],
        compiler_params=pltpu.CompilerParams(vmem_limit_bytes=MOST),
        cost_estimate=pl.CostEstimate(flops=2 << 30, bytes_accessed=10 << 20, transcendentals=0),
        name="own_product",
    )(block, own, other, out_weight, other_weight, top_more, bottom_more)


def finish_kernel(top_ref, bottom_ref, top_more_ref, bottom_more_ref, out_ref):
    out_ref[:ROWS] = (top_ref[...] + top_more_ref[...].astype(F32)).astype(BF16)
    out_ref[ROWS:] = (bottom_ref[...] + bottom_more_ref[...].astype(F32)).astype(BF16)


def finish(top, bottom, top_more, bottom_more):
    return pl.pallas_call(
        finish_kernel,
        in_specs=[HELD] * 4,
        out_shape=jax.ShapeDtypeStruct((2 * ROWS, top.shape[1]), BF16),
        compiler_params=pltpu.CompilerParams(vmem_limit_bytes=LITTLE),
        name="finish",
    )(top, bottom, top_more, bottom_more)


def chip_shift(array, step):
    return lax.ppermute(array, "tp", [(i, (i + 2 * step) % 8) for i in range(8)])


def core_swap(array):
    return lax.ppermute(array, "tp", [(i, i ^ 1) for i in range(8)])


def block_of(step):
    place = lax.axis_index("tp")
    return 2 * ((place // 2 + step) % 4) + place % 2


def far_weights(out_weight, other_weight):
    width = out_weight.shape[1] // 8
    start = block_of(2) * width
    return [lax.dynamic_slice_in_dim(w, start, width, 1) for w in (out_weight, other_weight)]


def project(gated, out_weight, other_weight, far):
    other = core_swap(gated)
    add = lambda a, b: (a.astype(F32) + b.astype(F32)).astype(BF16)
    far_top, far_bottom = far_product(far_own_product(gated, far[0]), other, far[1])
    up = chip_shift(far_top, 1)
    down = chip_shift(far_bottom, -1)
    near = jnp.stack([block_of(1), block_of(3)])
    next_top, next_bottom, last_top, last_bottom = near_product(
        gated, other, out_weight, other_weight, near
    )
    up_direct = chip_shift(next_bottom, 1)
    down_direct = chip_shift(last_top, -1)
    up_sum = chip_shift(add(next_top, up), 1)
    down_sum = chip_shift(add(last_bottom, down), -1)
    top, bottom = own_product(
        gated, other, out_weight, other_weight, block_of(0).reshape(1), down_direct, up_direct
    )
    return finish(top, bottom, up_sum, down_sum)


def convolve(key_proj, value_proj, filter_spectrum, early=()):
    first, last, forward, backward, turn, side = tables()
    as_bf16 = lambda t: jnp.asarray(t.astype(np.float32)).astype(BF16)
    waves = np.concatenate([turn[:, :, :16], side.reshape(2, 16, 16, 128).swapaxes(0, 1)])
    waves = jnp.asarray(waves.astype(np.float32))
    turn = jnp.asarray(np.concatenate([turn, side[None]]).astype(np.float32))
    signal = pack_signal(key_proj, value_proj)
    signal = lax.all_to_all(signal, "ctx", split_axis=0, concat_axis=0, tiled=True)
    spectrum = pack_spectrum(filter_spectrum, as_bf16(shuffles()))
    signal, spectrum = lax.optimization_barrier((signal, spectrum))
    spectrum = lax.all_to_all(spectrum, "ctx", split_axis=0, concat_axis=0, tiled=True)
    x = forward_part(signal, as_bf16(first), as_bf16(forward), turn)
    x, *early = lax.optimization_barrier((x, *early))
    out = filter_part(x, spectrum, as_bf16(np.concatenate([backward, last])), waves)
    return lax.all_to_all(out, "ctx", split_axis=0, concat_axis=0, tiled=True), early


def per_device(query_proj, key_proj, value_proj, filter_spectrum, skip_gain, out_weight):
    other_weight = core_swap(out_weight)
    far = far_weights(out_weight, other_weight)
    filtered, far = convolve(key_proj, value_proj, filter_spectrum, far)
    gated = gate(query_proj, key_proj, value_proj, skip_gain, filtered)
    return project(gated, out_weight, other_weight, far)


def solution(mesh):
    in_specs = (
        P("ctx", "tp"),
        P("ctx", "tp"),
        P("ctx", "tp"),
        P(None, "ctx", "tp"),
        P("tp"),
        P("tp", None),
    )
    out_specs = P("ctx", "tp")
    return jax.shard_map(
        per_device, mesh=mesh, in_specs=in_specs, out_specs=out_specs, check_vma=False
    )
```

```python
import functools
import math

import numpy as np

import jax
import jax.numpy as jnp
from jax import lax
from jax.experimental import pallas as pl
from jax.experimental.pallas import tpu as pltpu
from jax.sharding import PartitionSpec as P

ROWS = 256
HALF = 17
HELD = pl.BlockSpec(memory_space=pltpu.VMEM)
FAR = pl.BlockSpec(memory_space=pltpu.HBM)
SCALARS = pl.BlockSpec(memory_space=pltpu.SMEM)
F32 = jnp.float32
BF16 = jnp.bfloat16
TIGHT = 46 * 1024 * 1024
BIG = 60 * 1024 * 1024
LITTLE = 24 * 1024 * 1024
MOST = 48 * 1024 * 1024


def tables():
    a = np.arange(16)
    e = np.arange(HALF)
    angle = 2.0 * np.pi * np.outer(e, a) / 32.0
    first = np.concatenate([np.cos(angle), -np.sin(angle[1:16])], axis=0)
    last = np.concatenate([np.cos(angle), -np.sin(angle[1:16])], axis=0).T
    eye = np.eye(16)
    first = np.kron(first, eye)
    last = np.kron(last, eye) / 16384.0
    r = np.arange(ROWS)
    angle = 2.0 * np.pi * (np.outer(r, r) % ROWS) / ROWS
    c, s = np.cos(angle), np.sin(angle)
    forward = np.block([[c, s], [-s, c]])
    backward = np.block([[c, -s], [s, c]])
    lane = np.arange(128) // 64
    place = 256 * lane[None, :] + r[:, None]
    angle = 2.0 * np.pi * ((e[:, None, None] * place[None]) % 16384) / 16384.0
    turn = np.stack([np.cos(angle), -np.sin(angle)], axis=1)
    angle = 2.0 * np.pi * (lane[None, :] * r[:, None]) / 512.0
    side = np.stack([np.cos(angle), -np.sin(angle)])
    return first, last, forward, backward, turn, side


def shuffles():
    index = np.arange(16)
    plain = np.zeros((256, 256))
    turned = np.zeros((256, 256))
    for e in range(16):
        plain[16 * e + index, 16 * index + e] = 1.0
        turned[16 * e + 15 - index, 16 * index + e] = 1.0
    return np.stack([plain, turned])


def low_lanes(shape):
    return lax.broadcasted_iota(jnp.int32, shape, len(shape) - 1) < 64


def interleave(top, bottom):
    low = low_lanes(top.shape)
    even = jnp.where(low, top, pltpu.roll(bottom, 64, 1))
    odd = jnp.where(low, pltpu.roll(top, 64, 1), bottom)
    return even, odd


def pack_signal_kernel(key_ref, value_ref, out_ref, keys, values, done):
    width = 256
    copies = []
    for n in range(4):
        lanes = pl.ds(width * n, width)
        pair = [
            pltpu.make_async_copy(source.at[:, lanes], target.at[:, lanes], done.at[m, n])
            for m, (source, target) in enumerate(((key_ref, keys), (value_ref, values)))
        ]
        for copy in pair:
            copy.start()
        copies.append(pair)
    for b in range(8):
        if b % 2 == 0:
            for copy in copies[b // 2]:
                copy.wait()
        lanes = slice(128 * b, 128 * b + 128)
        for r in range(0, ROWS, 32):
            halves = []
            for n in range(2):
                rows = slice(ROWS * n + r, ROWS * n + r + 32)
                halves.append(keys[rows, lanes].astype(F32) * values[rows, lanes].astype(F32))
            even, odd = interleave(*halves)
            out_ref[2 * b, r : r + 32] = even.astype(BF16)
            out_ref[2 * b + 1, r : r + 32] = odd.astype(BF16)


def pack_signal(key_proj, value_proj):
    return pl.pallas_call(
        pack_signal_kernel,
        in_specs=[FAR] * 2,
        out_specs=HELD,
        out_shape=jax.ShapeDtypeStruct((16, ROWS, 128), BF16),
        scratch_shapes=[
            pltpu.VMEM(key_proj.shape, BF16),
            pltpu.VMEM(key_proj.shape, BF16),
            pltpu.SemaphoreType.DMA((2, 4)),
        ],
        compiler_params=pltpu.CompilerParams(vmem_limit_bytes=BIG),
        cost_estimate=pl.CostEstimate(flops=1 << 20, bytes_accessed=3 << 20, transcendentals=0),
        name="pack_signal",
    )(key_proj, value_proj)


def slot(e):
    if e == 16:
        return 1
    return 2 * e if e < 16 else 2 * (32 - e) + 1


def pack_spectrum_kernel(shuffle_ref, spec_ref, out_ref):
    width = 256
    for which in range(2):
        for start in range(0, spec_ref.shape[2], width):
            rows = spec_ref[which, :, start : start + width].reshape(16, 2, 2, 16, width)
            for high in range(2):
                parts = []
                for g in range(2):
                    part = rows[:, g, high].reshape(256, width)
                    parts.append(jnp.dot(shuffle_ref[high], part, preferred_element_type=F32))
                if high:
                    parts = parts[::-1]
                for b in range(width // 128):
                    lanes = slice(128 * b, 128 * b + 128)
                    even, odd = interleave(parts[0][:, lanes], parts[1][:, lanes])
                    to = start // 64 + 2 * b
                    for e in range(16):
                        keep = slice(16 * e, 16 * e + 16)
                        out_ref[to, which, slot(16 * high + e)] = even[keep].astype(BF16)
                        out_ref[to + 1, which, slot(16 * high + e)] = odd[keep].astype(BF16)


def pack_spectrum(filter_spectrum, shuffle):
    return pl.pallas_call(
        pack_spectrum_kernel,
        in_specs=[HELD] * 2,
        out_specs=HELD,
        out_shape=jax.ShapeDtypeStruct((16, 2, 32, 16, 128), BF16),
        compiler_params=pltpu.CompilerParams(vmem_limit_bytes=LITTLE),
        cost_estimate=pl.CostEstimate(flops=1 << 30, bytes_accessed=12 << 20, transcendentals=0),
        name="pack_spectrum",
    )(shuffle, filter_spectrum)


def sign_lanes(shape):
    return jnp.where(low_lanes(shape), 1.0, -1.0).astype(F32)


def forward_kernel(first_ref, forward_ref, turn_ref, signal_ref, out_ref, part):
    side_ref = turn_ref.at[HALF]
    sign = sign_lanes((16, 128))

    def step(q, carry):
        at = pl.ds(pl.multiple_of(16 * q, 16), 16)
        block = signal_ref[:, at, :].reshape(256, 128)
        sums = jnp.dot(first_ref[...], block, preferred_element_type=F32).reshape(32, 16, 128)
        side_re = side_ref[0, at, :]
        side_im = side_ref[1, at, :]
        for e in range(HALF):
            re = sums[e]
            cos = turn_ref[e, 0, at, :]
            sin = turn_ref[e, 1, at, :]
            if e in (0, 16):
                c_re, c_im = re * cos, re * sin
            else:
                im = sums[16 + e]
                c_re, c_im = re * cos - im * sin, re * sin + im * cos
            d_re = c_re * sign + pltpu.roll(c_re, 64, 1)
            d_im = c_im * sign + pltpu.roll(c_im, 64, 1)
            part[e, 0, at, :] = (d_re * side_re - d_im * side_im).astype(BF16)
            part[e, 1, at, :] = (d_re * side_im + d_im * side_re).astype(BF16)
        return carry

    lax.fori_loop(0, 16, step, 0)

    def pair(n, carry):
        data = jnp.concatenate(
            [part[2 * n].reshape(512, 128), part[2 * n + 1].reshape(512, 128)], axis=1
        )
        x = jnp.dot(forward_ref[...], data, preferred_element_type=F32).astype(BF16)
        out_ref[2 * n] = x[:, :128].reshape(2, ROWS, 128)
        out_ref[2 * n + 1] = x[:, 128:].reshape(2, ROWS, 128)
        return carry

    lax.fori_loop(0, 8, pair, 0)
    x = jnp.dot(forward_ref[...], part[16].reshape(512, 128), preferred_element_type=F32)
    out_ref[16] = x.astype(BF16).reshape(2, ROWS, 128)


def forward_part(signal, first, forward, turn):
    return pl.pallas_call(
        forward_kernel,
        in_specs=[HELD] * 4,
        out_specs=HELD,
        out_shape=jax.ShapeDtypeStruct((HALF, 2, ROWS, 128), BF16),
        scratch_shapes=[pltpu.VMEM((HALF, 2, ROWS, 128), BF16)],
        compiler_params=pltpu.CompilerParams(vmem_limit_bytes=MOST),
        cost_estimate=pl.CostEstimate(flops=2 << 30, bytes_accessed=12 << 20, transcendentals=0),
        name="forward_part",
    )(first, forward, turn, signal)


def filter_kernel(
    tables_from,
    waves_from,
    x_ref,
    spec_ref,
    out_ref,
    tables_ref,
    waves_ref,
    held,
    products,
    sums,
    table_done,
):
    backward_ref = tables_ref.at[: 2 * ROWS]
    last_ref = tables_ref.at[2 * ROWS :]
    copies = [
        pltpu.make_async_copy(source.at[some], target.at[some], table_done.at[n])
        for n, (source, target, some) in enumerate(
            (
                (tables_from, tables_ref, pl.ds(0, 2 * ROWS)),
                (waves_from, waves_ref, pl.ds(0, HALF + 16)),
                (tables_from, tables_ref, pl.ds(2 * ROWS, ROWS)),
            )
        )
    ]
    for copy in copies:
        copy.start()
    sign = sign_lanes((16, 128))

    def spectrum(j, which, place):
        return spec_ref[j, which, place].astype(F32)

    def filter_at(e, j):
        if e == 0:
            return spectrum(j, 0, 0), spectrum(j, 1, 0)
        if e == 16:
            return spectrum(15 - j, 0, 1), -spectrum(15 - j, 1, 1)
        h_re = spectrum(j, 0, 2 * e) + spectrum(15 - j, 0, 2 * e + 1)
        h_im = spectrum(j, 1, 2 * e) - spectrum(15 - j, 1, 2 * e + 1)
        return h_re, h_im

    for start in range(0, HALF, 2):
        group = range(start, min(start + 2, HALF))
        for n, e in enumerate(group):
            lanes = slice(128 * n, 128 * n + 128)
            for j in range(16):
                rows = slice(16 * j, 16 * j + 16)
                below = slice(ROWS + 16 * j, ROWS + 16 * j + 16)
                h_re, h_im = filter_at(e, j)
                x_re, x_im = x_ref[e, 0, rows].astype(F32), x_ref[e, 1, rows].astype(F32)
                products[start // 2, rows, lanes] = (x_re * h_re - x_im * h_im).astype(BF16)
                products[start // 2, below, lanes] = (x_re * h_im + x_im * h_re).astype(BF16)
        wide = 128 * len(group)
        if start == 0:
            copies[0].wait()
        sums[start // 2, :, :wide] = jnp.dot(
            backward_ref[...], products[start // 2, :, :wide], preferred_element_type=F32
        )
        if start == 0:
            copies[1].wait()
        for n, e in enumerate(group):
            base_re, base_im = waves_ref[e, 0], waves_ref[e, 1]
            lanes = slice(128 * n, 128 * n + 128)
            for j in range(16):
                rows = slice(16 * j, 16 * j + 16)
                below = slice(ROWS + 16 * j, ROWS + 16 * j + 16)
                b_re = sums[start // 2, rows, lanes]
                b_im = sums[start // 2, below, lanes]
                side_re, side_im = waves_ref[HALF + j, 0], waves_ref[HALF + j, 1]
                s_re = b_re * side_re + b_im * side_im
                s_im = b_im * side_re - b_re * side_im
                c_re = s_re * sign + pltpu.roll(s_re, 64, 1)
                c_im = s_im * sign + pltpu.roll(s_im, 64, 1)
                angle = 2.0 * math.pi * (16 * j * e % 16384) / 16384.0
                step_re, step_im = math.cos(angle), -math.sin(angle)
                cos = base_re * step_re - base_im * step_im
                sin = base_re * step_im + base_im * step_re
                held[e, rows] = (c_re * cos + c_im * sin).astype(BF16)
                if e not in (0, 16):
                    held[16 + e, rows] = (c_im * cos - c_re * sin).astype(BF16)

    copies[2].wait()
    for q in range(0, 16, 2):
        block = jnp.concatenate(
            [held[:, 16 * p : 16 * p + 16].reshape(512, 128) for p in (q, q + 1)], axis=1
        )
        y = jnp.dot(last_ref[...], block, preferred_element_type=F32).astype(BF16)
        for n in range(2):
            out_ref[:, 16 * (q + n) : 16 * (q + n) + 16] = y[:, 128 * n : 128 * n + 128].reshape(
                16, 16, 128
            )


def filter_part(x, spectrum, tables, waves):
    return pl.pallas_call(
        filter_kernel,
        in_specs=[FAR] * 2 + [HELD] * 2,
        out_specs=HELD,
        out_shape=jax.ShapeDtypeStruct((16, ROWS, 128), BF16),
        scratch_shapes=[
            *[pltpu.VMEM(t.shape, t.dtype) for t in (tables, waves)],
            pltpu.VMEM((32, ROWS, 128), BF16),
            pltpu.VMEM((9, 2 * ROWS, 256), BF16),
            pltpu.VMEM((9, 2 * ROWS, 256), F32),
            pltpu.SemaphoreType.DMA((3,)),
        ],
        compiler_params=pltpu.CompilerParams(vmem_limit_bytes=TIGHT),
        cost_estimate=pl.CostEstimate(flops=2 << 30, bytes_accessed=16 << 20, transcendentals=0),
        name="filter_part",
    )(tables, waves, x, spectrum)


def gate_kernel(query_ref, key_ref, value_ref, skip_ref, filtered_ref, out_ref):
    for b in range(query_ref.shape[1] // 128):
        lanes = slice(128 * b, 128 * b + 128)
        skip = skip_ref[:, lanes]
        for r in range(0, ROWS, 32):
            halves = interleave(
                filtered_ref[2 * b, r : r + 32].astype(F32),
                filtered_ref[2 * b + 1, r : r + 32].astype(F32),
            )
            for n, filtered in enumerate(halves):
                rows = slice(ROWS * n + r, ROWS * n + r + 32)
                signal = key_ref[rows, lanes].astype(F32) * value_ref[rows, lanes].astype(F32)
                signal = signal.astype(BF16).astype(F32)
                held = filtered + skip * signal
                out_ref[rows, lanes] = (query_ref[rows, lanes].astype(F32) * held).astype(BF16)


def gate(query_proj, key_proj, value_proj, skip_gain, filtered):
    rows, channels = query_proj.shape
    return pl.pallas_call(
        gate_kernel,
        in_specs=[HELD] * 5,
        out_specs=HELD,
        out_shape=jax.ShapeDtypeStruct((rows, channels), BF16),
        compiler_params=pltpu.CompilerParams(vmem_limit_bytes=LITTLE),
        cost_estimate=pl.CostEstimate(flops=4 << 20, bytes_accessed=5 << 20, transcendentals=0),
        name="gate",
    )(query_proj, key_proj, value_proj, skip_gain.reshape(1, channels), filtered)


def far_own_kernel(own_ref, weight_ref, out_ref):
    out_ref[...] = jnp.dot(own_ref[...], weight_ref[...], preferred_element_type=F32)


def far_kernel(own_ref, other_ref, weight_ref, top_ref, bottom_ref):
    width = 256
    for start in range(0, weight_ref.shape[1], width):
        lanes = slice(start, start + width)
        total = own_ref[:, lanes]
        total += jnp.dot(other_ref[...], weight_ref[:, lanes], preferred_element_type=F32)
        top_ref[:, lanes] = total[:ROWS].astype(BF16)
        bottom_ref[:, lanes] = total[ROWS:].astype(BF16)


def far_own_product(own, weight):
    return pl.pallas_call(
        far_own_kernel,
        in_specs=[HELD] * 2,
        out_specs=HELD,
        out_shape=jax.ShapeDtypeStruct((own.shape[0], weight.shape[1]), F32),
        compiler_params=pltpu.CompilerParams(vmem_limit_bytes=LITTLE),
        cost_estimate=pl.CostEstimate(flops=1 << 30, bytes_accessed=5 << 20, transcendentals=0),
        name="far_own_product",
    )(own, weight)


def far_product(own, other, weight):
    shape = jax.ShapeDtypeStruct((ROWS, weight.shape[1]), BF16)
    return pl.pallas_call(
        far_kernel,
        in_specs=[HELD] * 3,
        out_specs=[HELD] * 2,
        out_shape=[shape, shape],
        compiler_params=pltpu.CompilerParams(vmem_limit_bytes=LITTLE),
        cost_estimate=pl.CostEstimate(flops=1 << 30, bytes_accessed=5 << 20, transcendentals=0),
        name="far_product",
    )(own, other, weight)


def near_kernel(place_ref, own_ref, other_ref, weight_ref, other_weight_ref, *refs):
    outs, (held, done) = refs[:4], refs[4:]
    columns = outs[0].shape[1]
    width = columns // 2
    steps = [(b, i) for b in range(2) for i in range(2)]
    arrivals = []
    for b, i in steps:
        at = pl.ds(pl.multiple_of(place_ref[b] * columns + width * i, width), width)
        arrivals.append(
            [
                pltpu.make_async_copy(w.at[:, at], held.at[b, i, m], done.at[b, i, m])
                for m, w in enumerate((weight_ref, other_weight_ref))
            ]
        )
    for copy in sum(arrivals, []):
        copy.start()
    for (b, i), pair in zip(steps, arrivals):
        for copy in pair:
            copy.wait()
        lanes = slice(width * i, width * i + width)
        total = jnp.dot(own_ref[...], held[b, i, 0], preferred_element_type=F32)
        total += jnp.dot(other_ref[...], held[b, i, 1], preferred_element_type=F32)
        outs[2 * b][:, lanes] = total[:ROWS].astype(BF16)
        outs[2 * b + 1][:, lanes] = total[ROWS:].astype(BF16)


def near_product(own, other, out_weight, other_weight, blocks):
    channels = own.shape[1]
    columns = out_weight.shape[1] // 8
    return pl.pallas_call(
        near_kernel,
        in_specs=[SCALARS] + [HELD] * 2 + [FAR] * 2,
        out_specs=[HELD] * 4,
        out_shape=[jax.ShapeDtypeStruct((ROWS, columns), BF16)] * 4,
        scratch_shapes=[
            pltpu.VMEM((2, 2, 2, channels, columns // 2), BF16),
            pltpu.SemaphoreType.DMA((2, 2, 2)),
        ],
        compiler_params=pltpu.CompilerParams(vmem_limit_bytes=MOST),
        cost_estimate=pl.CostEstimate(flops=4 << 30, bytes_accessed=10 << 20, transcendentals=0),
        name="near_product",
    )(blocks, own, other, out_weight, other_weight)


def own_kernel(
    place_ref,
    own_ref,
    other_ref,
    weight_ref,
    other_weight_ref,
    top_more_ref,
    bottom_more_ref,
    top_ref,
    bottom_ref,
):
    total = jnp.dot(own_ref[...], weight_ref[...], preferred_element_type=F32)
    total += jnp.dot(other_ref[...], other_weight_ref[...], preferred_element_type=F32)
    top_ref[...] = total[:ROWS] + top_more_ref[...].astype(F32)
    bottom_ref[...] = total[ROWS:] + bottom_more_ref[...].astype(F32)


def own_product(own, other, out_weight, other_weight, block, top_more, bottom_more):
    rows, channels = own.shape
    columns = out_weight.shape[1] // 8
    width = 512
    steps = columns // width
    data = pl.BlockSpec((rows, channels), lambda i, at: (0, 0))
    weight = pl.BlockSpec((channels, width), lambda i, at: (0, at[0] * steps + i))
    half = pl.BlockSpec((ROWS, width), lambda i, at: (0, i))
    shape = jax.ShapeDtypeStruct((ROWS, columns), F32)
    return pl.pallas_call(
        own_kernel,
        grid_spec=pltpu.PrefetchScalarGridSpec(
            num_scalar_prefetch=1,
            grid=(steps,),
            in_specs=[data, data, weight, weight, half, half],
            out_specs=[half, half],
        ),
        out_shape=[shape, shape],
        compiler_params=pltpu.CompilerParams(vmem_limit_bytes=MOST),
        cost_estimate=pl.CostEstimate(flops=2 << 30, bytes_accessed=10 << 20, transcendentals=0),
        name="own_product",
    )(block, own, other, out_weight, other_weight, top_more, bottom_more)


def finish_kernel(own_ref, sum_ref, *refs):
    refs[-1][...] = (own_ref[...] + sum_ref[...].astype(F32)).astype(BF16)


def finish(own, summed, half, out=None):
    rows, columns = own.shape
    part = pl.BlockSpec((rows // 2, columns), lambda i: (i, 0))
    given = [] if out is None else [out]
    return pl.pallas_call(
        finish_kernel,
        grid=(2,),
        in_specs=[part] * 2 + [pl.BlockSpec(memory_space=pl.ANY)] * len(given),
        out_specs=pl.BlockSpec((rows // 2, columns), lambda i: (2 * half + i, 0)),
        out_shape=jax.ShapeDtypeStruct((2 * rows, columns), BF16),
        input_output_aliases={2: 0} if given else {},
        compiler_params=pltpu.CompilerParams(vmem_limit_bytes=LITTLE),
        name="finish",
    )(own, summed, *given)


def chip_shift(array, step):
    return lax.ppermute(array, "tp", [(i, (i + 2 * step) % 8) for i in range(8)])


def core_swap(array):
    return lax.ppermute(array, "tp", [(i, i ^ 1) for i in range(8)])


def block_of(step):
    place = lax.axis_index("tp")
    return 2 * ((place // 2 + step) % 4) + place % 2


def far_weights(out_weight, other_weight):
    width = out_weight.shape[1] // 8
    start = block_of(2) * width
    return [lax.dynamic_slice_in_dim(w, start, width, 1) for w in (out_weight, other_weight)]


def project(gated, out_weight, other_weight, far):
    other = core_swap(gated)
    add = lambda a, b: (a.astype(F32) + b.astype(F32)).astype(BF16)
    far_top, far_bottom = far_product(far_own_product(gated, far[0]), other, far[1])
    up = chip_shift(far_top, 1)
    down = chip_shift(far_bottom, -1)
    near = jnp.stack([block_of(1), block_of(3)])
    next_top, next_bottom, last_top, last_bottom = near_product(
        gated, other, out_weight, other_weight, near
    )
    up_direct = chip_shift(next_bottom, 1)
    down_direct = chip_shift(last_top, -1)
    up_sum = chip_shift(add(next_top, up), 1)
    down_sum = chip_shift(add(last_bottom, down), -1)
    top, bottom = own_product(
        gated, other, out_weight, other_weight, block_of(0).reshape(1), down_direct, up_direct
    )
    out = finish(bottom, down_sum, 1)
    return finish(top, up_sum, 0, out)


def convolve(key_proj, value_proj, filter_spectrum, early=()):
    first, last, forward, backward, turn, side = tables()
    as_bf16 = lambda t: jnp.asarray(t.astype(np.float32)).astype(BF16)
    waves = np.concatenate([turn[:, :, :16], side.reshape(2, 16, 16, 128).swapaxes(0, 1)])
    waves = jnp.asarray(waves.astype(np.float32))
    turn = jnp.asarray(np.concatenate([turn, side[None]]).astype(np.float32))
    signal = pack_signal(key_proj, value_proj)
    signal = lax.all_to_all(signal, "ctx", split_axis=0, concat_axis=0, tiled=True)
    spectrum = pack_spectrum(filter_spectrum, as_bf16(shuffles()))
    signal, spectrum = lax.optimization_barrier((signal, spectrum))
    spectrum = lax.all_to_all(spectrum, "ctx", split_axis=0, concat_axis=0, tiled=True)
    x = forward_part(signal, as_bf16(first), as_bf16(forward), turn)
    x, *early = lax.optimization_barrier((x, *early))
    out = filter_part(x, spectrum, as_bf16(np.concatenate([backward, last])), waves)
    return lax.all_to_all(out, "ctx", split_axis=0, concat_axis=0, tiled=True), early


def per_device(query_proj, key_proj, value_proj, filter_spectrum, skip_gain, out_weight):
    other_weight = core_swap(out_weight)
    far = far_weights(out_weight, other_weight)
    filtered, far = convolve(key_proj, value_proj, filter_spectrum, far)
    gated = gate(query_proj, key_proj, value_proj, skip_gain, filtered)
    return project(gated, out_weight, other_weight, far)


def solution(mesh):
    in_specs = (
        P("ctx", "tp"),
        P("ctx", "tp"),
        P("ctx", "tp"),
        P(None, "ctx", "tp"),
        P("tp"),
        P("tp", None),
    )
    out_specs = P("ctx", "tp")
    return jax.shard_map(
        per_device, mesh=mesh, in_specs=in_specs, out_specs=out_specs, check_vma=False
    )
```
